128 devices in a mesh: row: 8 (over y, core), col: 16 (over x, z).
Axes of the slice: x: 4, y: 4, z: 4, core: 2. Of those that a mesh axis runs over, the one named last changes fastest.
Arguments:
- tokens: bfloat16 [512, 8192], P('row', 'col'), may hold values from -6 to 6
- w_gate: bfloat16 [8192, 28672], P('col', 'row'), may hold values from -0.0625 to 0.0625
- w_up: bfloat16 [8192, 28672], P('col', 'row'), may hold values from -0.0625 to 0.0625
- w_down: bfloat16 [28672, 8192], P('row', 'col'), may hold values from -0.03125 to 0.03125
- cotangent: bfloat16 [512, 8192], P('row', 'col'), may hold values from -1.1953125 to 1.1953125
Outputs:
- mixed: bfloat16 [512, 8192], P('row', 'col')
- input_grad: bfloat16 [512, 8192], P('row', 'col')
- gate_wgrad: bfloat16 [8192, 28672], P('col', 'row')
- up_wgrad: bfloat16 [8192, 28672], P('col', 'row')
- down_wgrad: bfloat16 [28672, 8192], P('row', 'col')
The draws below stay inside these ranges and needn't reach their ends.
All inputs are finite; a program needn't handle non-finite values.
Results may differ from the reference program's by a relative error of at most 0.005.
Values may be sent and summed in bfloat16 or wider, within the bound.
A program may use at most 128 MiB of HBM per device.

```python
import jax
import jax.numpy as jnp

D = 8192
FF = 28672
TOKENS = 512


def level_of(stream_key, extent, shards, smallest, top_value):
    factor_of = 1.0
    for axis_at, parts in shards:
        steps = jax.random.uniform(jax.random.fold_in(jax.random.fold_in(stream_key, 6), axis_at), (parts,), jnp.float32, smallest / len(shards), top_value / len(shards))
        factor_of = factor_of * jnp.repeat(jnp.exp(steps), extent[axis_at] // parts).reshape((-1,) + (1,) * (len(extent) - 1 - axis_at))
    return factor_of


def noise(key, extent, spread, bound, cuts=(), dtype=jnp.bfloat16):
    values = spread * jax.random.normal(key, extent, jnp.float32)
    if cuts:
        values = values * level_of(key, extent, cuts, -0.22, 0.18)
    return jnp.clip(values, -bound, bound).astype(dtype)


def setup_inputs(seed: int = 0) -> dict:
    streams_of = jax.random.split(jax.random.key(seed), 6)
    return {
        "tokens": noise(streams_of[0], (TOKENS, D), 1.0, 6.0, ((0, 8), (1, 16))),
        "w_gate": noise(streams_of[1], (D, FF), D ** -0.5, 0.0625, ((0, 16), (1, 8))),
        "w_up": noise(streams_of[2], (D, FF), D ** -0.5, 0.0625, ((0, 16), (1, 8))),
        "w_down": noise(streams_of[3], (FF, D), FF ** -0.5, 0.03125, ((0, 8), (1, 16))),
        "cotangent": noise(streams_of[4], (TOKENS, D), 0.2, 1.1953125, ((0, 8), (1, 16))),
    }


def reference(tokens, w_gate, w_up, w_down, cotangent):
    gate = jnp.dot(tokens, w_gate, preferred_element_type=jnp.float32)
    up = jnp.dot(tokens, w_up, preferred_element_type=jnp.float32)
    activated = jax.nn.silu(gate)
    hidden = (activated * up).astype(jnp.bfloat16)
    mixed = jnp.dot(hidden, w_down, preferred_element_type=jnp.float32).astype(jnp.bfloat16)
    hidden_grad = jnp.dot(cotangent, w_down.T, preferred_element_type=jnp.float32)
    sigmoid_gate = jax.nn.sigmoid(gate)
    gate_grad = (hidden_grad * up * sigmoid_gate * (1.0 + gate * (1.0 - sigmoid_gate))).astype(jnp.bfloat16)
    up_grad = (hidden_grad * activated).astype(jnp.bfloat16)
    down_wgrad = jnp.dot(hidden.T, cotangent, preferred_element_type=jnp.float32).astype(jnp.bfloat16)
    gate_wgrad = jnp.dot(tokens.T, gate_grad, preferred_element_type=jnp.float32).astype(jnp.bfloat16)
    up_wgrad = jnp.dot(tokens.T, up_grad, preferred_element_type=jnp.float32).astype(jnp.bfloat16)
    input_sum = jnp.dot(gate_grad, w_gate.T, preferred_element_type=jnp.float32) + jnp.dot(up_grad, w_up.T, preferred_element_type=jnp.float32)
    input_grad = input_sum.astype(jnp.bfloat16)
    return mixed, input_grad, gate_wgrad, up_wgrad, down_wgrad
```

```python
import jax
import jax.numpy as jnp
from jax import lax
from jax.experimental import pallas as pl
from jax.experimental.pallas import tpu as pltpu
from jax.sharding import PartitionSpec as P

MESH = pl.DeviceIdType.MESH
BF16 = jnp.bfloat16
F32 = jnp.float32
WIDTH = 256
DEPTH = 8

FAR_UP, FAR_DOWN, OWN_UP, OWN_DOWN, SUM_UP, SUM_DOWN = range(6)
SECOND = 6
GIVE_UP, GIVE_DOWN, PASS_UP, PASS_DOWN = range(12, 16)
WIDE_UP, WIDE_DOWN, WIDE_PASS_UP, WIDE_PASS_DOWN = range(16, 20)
COPIES = 20


def dot(left, right):
    return jnp.dot(left, right, preferred_element_type=F32)


def dot_nt(left, right):
    return lax.dot_general(left, right, (((1,), (1,)), ((), ())), preferred_element_type=F32)


def ring_kernel(
    steps,
    tok_ref, cot_ref, wg_hbm, wu_hbm, wd_hbm,
    hid_out, gg_out, ug_out, tok_out, cot_out, mi_out,
    wg, wu, wd, nat, perm, far, far_in, near, near_in,
    far2, far2_in, near2, near2_in, sub, all3, acc, core_in, y_send, y_in,
    send_sem, recv_sem, w_sem, out_sem, g_send, g_recv, r_send, r_recv, tok_sem,
):
    row, col = lax.axis_index("row"), lax.axis_index("col")
    x, z, y, core = col // 4, col % 4, row // 2, row % 2
    width = WIDTH

    def at_x(i):
        return (row, lax.rem(i, 4) * 4 + z)

    def at_z(i):
        return (row, x * 4 + lax.rem(i, 4))

    def at_y(i):
        return (lax.rem(i, 4) * 2 + core, col)

    sibling = (row + 1 - 2 * core, col)
    rings = ((x, z, at_x, at_z), (z, x, at_z, at_x))

    for k in range(steps):
        cols = pl.ds(k * 2 * width, 2 * width)
        pltpu.make_async_copy(wd_hbm.at[cols, :], wd.at[k], w_sem.at[k, 2]).start()
        pltpu.make_async_copy(wg_hbm.at[:, cols], wg.at[k], w_sem.at[k, 0]).start()
        pltpu.make_async_copy(wu_hbm.at[:, cols], wu.at[k], w_sem.at[k, 1]).start()

    for half in range(2):
        nat[0, y, 2 * core + half] = tok_ref[32 * half : 32 * half + 32, :]
        nat[1, y, 2 * core + half] = cot_ref[32 * half : 32 * half + 32, :]

    barrier = pltpu.get_barrier_semaphore()
    peers = [at_x(x + 1), at_x(x + 3), at_z(z + 1), at_z(z + 3), at_y(y + 1), at_y(y + 2), at_y(y + 3), sibling]
    for peer in peers:
        pl.semaphore_signal(barrier, inc=1, device_id=peer, device_id_type=MESH)
    pl.semaphore_wait(barrier, len(peers))

    def rows_of(y_at, core_at):
        return nat.at[:, y_at, pl.ds(2 * core_at, 2)]

    def y_copy(step):
        return pltpu.make_async_remote_copy(
            src_ref=rows_of(y, core), dst_ref=rows_of(y, core), send_sem=g_send.at[step], recv_sem=g_recv.at[step],
            device_id=at_y(y + step), device_id_type=MESH,
        )

    def y_arrival(step):
        came = lax.rem(y + 4 - step, 4)
        return pltpu.make_async_remote_copy(
            src_ref=rows_of(came, core), dst_ref=rows_of(came, core), send_sem=g_send.at[step],
            recv_sem=g_recv.at[step], device_id=at_y(y + step), device_id_type=MESH,
        )

    def core_copy(step, core_at):
        came = lax.rem(y + 4 - step, 4)
        return pltpu.make_async_remote_copy(
            src_ref=rows_of(came, core_at), dst_ref=rows_of(came, core_at), send_sem=g_send.at[4 + step],
            recv_sem=g_recv.at[4 + step], device_id=sibling, device_id_type=MESH,
        )

    for step in (2, 1, 3):
        y_copy(step).start()
    core_copy(0, core).start()
    for step in (1, 3, 2):
        y_arrival(step).wait_recv()
        core_copy(step, core).start()
    for step in range(4):
        core_copy(step, 1 - core).wait_recv()
    for step in (1, 2, 3):
        y_copy(step).wait_send()
    for step in range(4):
        core_copy(step, core).wait_send()

    for i in range(4):
        for j in range(4):
            perm[:, j, i] = nat[:, i, j]
    keep = (
        pltpu.make_async_copy(nat.at[0], tok_out, tok_sem.at[0]),
        pltpu.make_async_copy(nat.at[1], cot_out, tok_sem.at[1]),
    )
    for copy in keep:
        copy.start()
    acc[...] = jnp.zeros_like(acc)

    def part(h, k, a, block, first, count):
        tokens = (nat, perm)[h]
        left = tokens[1 if a == 2 else 0, block, pl.ds(first, count)].reshape(count * 32, -1)
        if a == 2:
            return dot_nt(left, wd[k, h * width : (h + 1) * width, :])
        return dot(left, (wg, wu)[a][k, :, h * width : (h + 1) * width])

    def copy_of(kind, k, h, src, dst, target):
        at = 2 * k + h
        return pltpu.make_async_remote_copy(
            src_ref=src, dst_ref=dst, send_sem=send_sem.at[at, kind], recv_sem=recv_sem.at[at, kind],
            device_id=target, device_id_type=MESH,
        )

    def copies(k, h):
        at = 2 * k + h
        p, q, at_p, at_q = rings[h]
        up, down, up2, down2 = at_p(p + 1), at_p(p + 3), at_q(q + 1), at_q(q + 3)
        q_up, q_down = lax.rem(q + 1, 4), lax.rem(q + 3, 4)
        p_up, p_down = lax.rem(p + 1, 4), lax.rem(p + 3, 4)
        table = {}

        def same(kind, src, dst, target):
            table[kind] = (src, dst, target, dst)

        for base, f, fi, n, ni, u, d in (
            (0, far, far_in, near, near_in, up, down),
            (SECOND, far2, far2_in, near2, near2_in, up2, down2),
        ):
            same(base + FAR_UP, f.at[at, 0], fi.at[at, 0], u)
            same(base + FAR_DOWN, f.at[at, 1], fi.at[at, 1], d)
            same(base + SUM_UP, n.at[at, 0, 0], ni.at[at, 0, 0], u)
            same(base + OWN_UP, n.at[at, 0, 1], ni.at[at, 0, 1], u)
            same(base + OWN_DOWN, n.at[at, 1, 0], ni.at[at, 1, 0], d)
            same(base + SUM_DOWN, n.at[at, 1, 1], ni.at[at, 1, 1], d)

        def held(kind, mine, theirs, target):
            table[kind] = (mine, mine, target, theirs)

        mine = all3.at[at, :, p, q]
        held(GIVE_UP, mine, all3.at[at, :, p, q_down], up2)
        held(GIVE_DOWN, mine, all3.at[at, :, p, q_up], down2)
        opp_q, opp_p = lax.rem(q + 2, 4), lax.rem(p + 2, 4)
        low, high = pl.ds(0, 16), pl.ds(16, 16)
        held(PASS_UP, all3.at[at, :, p, q_down, low], all3.at[at, :, p, opp_q, low], up2)
        held(PASS_DOWN, all3.at[at, :, p, q_up, high], all3.at[at, :, p, opp_q, high], down2)
        held(WIDE_UP, all3.at[at, :, p], all3.at[at, :, p_down], up)
        held(WIDE_DOWN, all3.at[at, :, p], all3.at[at, :, p_up], down)
        low, high = pl.ds(0, 2), pl.ds(2, 2)
        held(WIDE_PASS_UP, all3.at[at, :, p_down, low], all3.at[at, :, opp_p, low], up)
        held(WIDE_PASS_DOWN, all3.at[at, :, p_up, high], all3.at[at, :, opp_p, high], down)
        return table

    def start(k, h, *kinds):
        table = copies(k, h)
        for kind in kinds:
            src, dst, target, _ = table[kind]
            copy_of(kind, k, h, src, dst, target).start()

    def arrive(k, h, *kinds):
        table = copies(k, h)
        for kind in kinds:
            src, _, target, here = table[kind]
            copy_of(kind, k, h, here, here, target).wait_recv()

    def sent(k, h):
        for kind, (src, dst, target, _) in copies(k, h).items():
            copy_of(kind, k, h, src, dst, target).wait_send()

    def stage0(k):
        cols = pl.ds(0, 2 * width)
        pltpu.make_async_copy(wd_hbm.at[cols, :], wd.at[k], w_sem.at[k, 2]).wait()
        pltpu.make_async_copy(wg_hbm.at[:, cols], wg.at[k], w_sem.at[k, 0]).wait()
        pltpu.make_async_copy(wu_hbm.at[:, cols], wu.at[k], w_sem.at[k, 1]).wait()
        for h in range(2):
            p = rings[h][0]
            at = 2 * k + h
            for a in range(3):
                whole = part(h, k, a, lax.rem(p + 2, 4), 0, 4).astype(BF16)
                far[at, 0, a] = whole[:64]
                far[at, 1, a] = whole[64:]
            start(k, h, FAR_UP, FAR_DOWN)
            for a in range(3):
                near[at, 0, 1, a] = part(h, k, a, lax.rem(p + 1, 4), 2, 2).astype(BF16)
                near[at, 1, 0, a] = part(h, k, a, lax.rem(p + 3, 4), 0, 2).astype(BF16)
            start(k, h, OWN_UP, OWN_DOWN)

    def stage1(k):
        for h in range(2):
            p = rings[h][0]
            at = 2 * k + h
            arrive(k, h, FAR_UP, FAR_DOWN)
            for a in range(3):
                near[at, 0, 0, a] = (
                    part(h, k, a, lax.rem(p + 1, 4), 0, 2) + far_in[at, 0, a].astype(F32)
                ).astype(BF16)
                near[at, 1, 1, a] = (
                    part(h, k, a, lax.rem(p + 3, 4), 2, 2) + far_in[at, 1, a].astype(F32)
                ).astype(BF16)
            start(k, h, SUM_UP, SUM_DOWN)

    def stage2(k):
        slot = lax.rem(k, 3)
        for h in range(2):
            p, q = rings[h][:2]
            at = 2 * k + h
            arrive(k, h, OWN_UP, OWN_DOWN, SUM_UP, SUM_DOWN)
            for a in range(3):
                for half in range(2):
                    total = (
                        part(h, k, a, p, 2 * half, 2)
                        + near_in[at, 0, half, a].astype(F32)
                        + near_in[at, 1, half, a].astype(F32)
                    )
                    sub[slot, h, a, 2 * half] = total[:32]
                    sub[slot, h, a, 2 * half + 1] = total[32:]
            for a in range(3):
                opposite = sub[slot, h, a, lax.rem(q + 2, 4)].astype(BF16)
                far2[at, 0, a] = opposite[:16]
                far2[at, 1, a] = opposite[16:]
                near2[at, 0, 1, a] = sub[slot, h, a, lax.rem(q + 1, 4), 16:, :].astype(BF16)
                near2[at, 1, 0, a] = sub[slot, h, a, lax.rem(q + 3, 4), :16, :].astype(BF16)
            start(k, h, *(SECOND + kind for kind in (FAR_UP, FAR_DOWN, OWN_UP, OWN_DOWN)))

    def stage3(k):
        slot = lax.rem(k, 3)
        for h in range(2):
            q = rings[h][1]
            at = 2 * k + h
            arrive(k, h, SECOND + FAR_UP, SECOND + FAR_DOWN)
            for a in range(3):
                near2[at, 0, 0, a] = (
                    sub[slot, h, a, lax.rem(q + 1, 4), :16, :] + far2_in[at, 0, a].astype(F32)
                ).astype(BF16)
                near2[at, 1, 1, a] = (
                    sub[slot, h, a, lax.rem(q + 3, 4), 16:, :] + far2_in[at, 1, a].astype(F32)
                ).astype(BF16)
            start(k, h, SECOND + SUM_UP, SECOND + SUM_DOWN)

    def stage4(k):
        slot = lax.rem(k, 3)
        for h in range(2):
            p, q = rings[h][:2]
            at = 2 * k + h
            arrive(k, h, *(SECOND + kind for kind in (OWN_UP, OWN_DOWN, SUM_UP, SUM_DOWN)))
            for half in range(2):
                rows = slice(16 * half, 16 * half + 16)
                gate, up, hidden_grad = (
                    sub[slot, h, a, q, rows, :]
                    + near2_in[at, 0, half, a].astype(F32)
                    + near2_in[at, 1, half, a].astype(F32)
                    for a in range(3)
                )
                sigmoid_gate = 1.0 / (1.0 + jnp.exp(-gate))
                activated = gate * sigmoid_gate
                all3[at, 0, p, q, rows, :] = (activated * up).astype(BF16)
                all3[at, 1, p, q, rows, :] = (
                    hidden_grad * up * sigmoid_gate * (1.0 + gate * (1.0 - sigmoid_gate))
                ).astype(BF16)
                all3[at, 2, p, q, rows, :] = (hidden_grad * activated).astype(BF16)
            start(k, h, GIVE_UP, GIVE_DOWN)

    def stage5(k):
        for h in range(2):
            arrive(k, h, GIVE_UP, GIVE_DOWN)
            start(k, h, PASS_UP, PASS_DOWN)

    def stage6(k):
        for h in range(2):
            arrive(k, h, PASS_UP, PASS_DOWN)
            start(k, h, WIDE_UP, WIDE_DOWN)

    def stage7(k):
        for h in range(2):
            arrive(k, h, WIDE_UP, WIDE_DOWN)
            start(k, h, WIDE_PASS_UP, WIDE_PASS_DOWN)

    def keeps(k):
        copies_out = []
        for h in range(2):
            at = 2 * k + h
            cols = pl.ds(pl.multiple_of(at * width, width), width)
            for a, out in enumerate((hid_out, gg_out, ug_out)):
                if h == 0:
                    copies_out.append((all3.at[at, a], out.at[:, :, :, cols], 5 * a))
                else:
                    for j in range(4):
                        copies_out.append((all3.at[at, a, j], out.at[:, j, :, cols], 5 * a + 1 + j))
        return [pltpu.make_async_copy(src, dst, out_sem.at[k, n]) for src, dst, n in copies_out]

    def stage8(k):
        for h in range(2):
            arrive(k, h, WIDE_PASS_UP, WIDE_PASS_DOWN)
        for copy in keeps(k):
            copy.start()
        for h in range(2):
            at = 2 * k + h
            sent(k, h)
            hidden_rows = slice(h * width, (h + 1) * width)
            for b in range(4):
                hidden, gate_grad, up_grad = (all3[at, a, b].reshape(128, width) for a in range(3))
                mixed = dot(hidden, wd[k, hidden_rows, :])
                into = dot_nt(gate_grad, wg[k, :, hidden_rows]) + dot_nt(up_grad, wu[k, :, hidden_rows])
                for j in range(4):
                    rows = slice(32 * j, 32 * j + 32)
                    i, jj = (b, j) if h == 0 else (j, b)
                    acc[0, i, jj] += mixed[rows]
                    acc[1, i, jj] += into[rows]

    stages = (stage0, stage1, stage2, stage3, stage4, stage5, stage6, stage7, stage8)

    def turn(i, carry):
        for late, stage in enumerate(stages):
            @pl.when((i >= late) & (i < steps + late))
            def _():
                stage(i - late)
        return carry

    lax.fori_loop(0, steps + DEPTH, turn, 0)

    def acc_rows(y_at, core_at):
        return acc.at[:, y_at, pl.ds(2 * core_at, 2)]

    def core_sum(step):
        return pltpu.make_async_remote_copy(
            src_ref=acc_rows(lax.rem(y + step, 4), 1 - core), dst_ref=core_in.at[step], send_sem=r_send.at[step],
            recv_sem=r_recv.at[step], device_id=sibling, device_id_type=MESH,
        )

    def y_sum(step):
        return pltpu.make_async_remote_copy(
            src_ref=y_send.at[step], dst_ref=y_in.at[step], send_sem=r_send.at[4 + step],
            recv_sem=r_recv.at[4 + step], device_id=at_y(y + step), device_id_type=MESH,
        )

    order = (2, 1, 3, 0)
    for step in order:
        core_sum(step).start()
    for step in order:
        core_sum(step).wait_recv()
        total = acc[:, lax.rem(y + step, 4), pl.ds(2 * core, 2)] + core_in[step]
        y_send[step] = total
        if step:
            y_sum(step).start()
    for step in (1, 3, 2):
        y_sum(step).wait_recv()
    result = y_send[0] + y_in[1] + y_in[2] + y_in[3]
    for j in range(2):
        mi_out[:, 32 * j : 32 * j + 32, :] = result[:, j].astype(BF16)
    for step in order:
        core_sum(step).wait_send()
        if step:
            y_sum(step).wait_send()

    for copy in keep:
        copy.wait()

    def finish(k, carry):
        for copy in keeps(k):
            copy.wait()
        return carry

    lax.fori_loop(0, steps, finish, 0)


def ring_call(tokens, w_gate, w_up, w_down, cotangent):
    features, hidden = w_gate.shape
    steps = hidden // (2 * WIDTH)
    parts = 2 * steps
    any_space = pl.BlockSpec(memory_space=pl.ANY)
    vmem = pl.BlockSpec(memory_space=pltpu.VMEM)

    def kernel(*refs):
        ring_kernel(steps, *refs)

    wide = jax.ShapeDtypeStruct((4, 4, 32, hidden), BF16)
    model = jax.ShapeDtypeStruct((4, 4, 32, features), BF16)
    dma = pltpu.SemaphoreType.DMA
    return pl.pallas_call(
        kernel,
        out_shape=(wide, wide, wide, model, model, jax.ShapeDtypeStruct((2, 64, features), BF16)),
        in_specs=[vmem, vmem, any_space, any_space, any_space],
        out_specs=(any_space,) * 5 + (vmem,),
        scratch_shapes=[
            pltpu.VMEM((steps, features, 2 * WIDTH), BF16),
            pltpu.VMEM((steps, features, 2 * WIDTH), BF16),
            pltpu.VMEM((steps, 2 * WIDTH, features), BF16),
            pltpu.VMEM((2, 4, 4, 32, features), BF16),
            pltpu.VMEM((2, 4, 4, 32, features), BF16),
            pltpu.VMEM((parts, 2, 3, 64, WIDTH), BF16),
            pltpu.VMEM((parts, 2, 3, 64, WIDTH), BF16),
            pltpu.VMEM((parts, 2, 2, 3, 64, WIDTH), BF16),
            pltpu.VMEM((parts, 2, 2, 3, 64, WIDTH), BF16),
            pltpu.VMEM((parts, 2, 3, 16, WIDTH), BF16),
            pltpu.VMEM((parts, 2, 3, 16, WIDTH), BF16),
            pltpu.VMEM((parts, 2, 2, 3, 16, WIDTH), BF16),
            pltpu.VMEM((parts, 2, 2, 3, 16, WIDTH), BF16),
            pltpu.VMEM((3, 2, 3, 4, 32, WIDTH), F32),
            pltpu.VMEM((parts, 3, 4, 4, 32, WIDTH), BF16),
            pltpu.VMEM((2, 4, 4, 32, features), F32),
            pltpu.VMEM((4, 2, 2, 32, features), F32),
            pltpu.VMEM((4, 2, 2, 32, features), F32),
            pltpu.VMEM((4, 2, 2, 32, features), F32),
            dma((parts, COPIES)),
            dma((parts, COPIES)),
            dma((steps, 3)),
            dma((steps, 15)),
            dma((8,)),
            dma((8,)),
            dma((8,)),
            dma((8,)),
            dma((2,)),
        ],
        name="ring_sums",
        compiler_params=pltpu.CompilerParams(
            collective_id=0, has_side_effects=True, vmem_limit_bytes=62 * 2**20
        ),
    )(tokens, cotangent, w_gate, w_up, w_down)


def matmul_tn(left, right):
    return lax.dot_general(left, right, (((0,), (0,)), ((), ())), preferred_element_type=F32).astype(BF16)


def shards(tokens, w_gate, w_up, w_down, cotangent):
    hidden, gate_grad, up_grad, tok_all, cot_all, sums = ring_call(tokens, w_gate, w_up, w_down, cotangent)
    hidden, gate_grad, up_grad, tok_all, cot_all = (
        a.reshape(512, a.shape[-1]) for a in (hidden, gate_grad, up_grad, tok_all, cot_all)
    )
    return (
        sums[0],
        sums[1],
        matmul_tn(tok_all, gate_grad),
        matmul_tn(tok_all, up_grad),
        matmul_tn(hidden, cot_all),
    )


def solution(mesh):
    return jax.shard_map(
        shards,
        mesh=mesh,
        in_specs=(P("row", "col"), P("col", "row"), P("col", "row"), P("row", "col"), P("row", "col")),
        out_specs=(P("row", "col"), P("row", "col"), P("col", "row"), P("col", "row"), P("row", "col")),
        check_vma=False,
    )
```

```python
import jax
import jax.numpy as jnp
from jax import lax
from jax.experimental import pallas as pl
from jax.experimental.pallas import tpu as pltpu
from jax.sharding import PartitionSpec as P

MESH = pl.DeviceIdType.MESH
BF16 = jnp.bfloat16
F32 = jnp.float32
WIDTH = 256
DEPTH = 8
EARLY = 4
AHEAD = 2
KEEP_PARTS = 2

FAR_UP, FAR_DOWN, OWN_UP, OWN_DOWN, SUM_UP, SUM_DOWN = range(6)
SECOND = 6
GIVE_UP, GIVE_DOWN, PASS_UP, PASS_DOWN = range(12, 16)
WIDE_UP, WIDE_DOWN, WIDE_PASS_UP, WIDE_PASS_DOWN = range(16, 20)
COPIES = 20


def dot(left, right):
    return jnp.dot(left, right, preferred_element_type=F32)


def dot_nt(left, right):
    return lax.dot_general(left, right, (((1,), (1,)), ((), ())), preferred_element_type=F32)


def dot_tn(left, right):
    return lax.dot_general(left, right, (((0,), (0,)), ((), ())), preferred_element_type=F32)


def ring_kernel(
    steps,
    tok_ref, cot_ref, wg_hbm, wu_hbm, wd_hbm,
    gg_out, ug_out, dg_out, own_out, sum1, sum2, sum3,
    wg, wu, wd, nat, perm, far, far_in, near, near_in,
    far2, far2_in, near2, near2_in, sub, all3, tok_t, grads, down_grads, acc, core_in, y_send, y_in,
    send_sem, recv_sem, w_sem, out_sem, g_send, g_recv, r_send, r_recv, y_sem, tok_sem,
):
    sum_outs = (own_out, sum1, sum2, sum3)
    row, col = lax.axis_index("row"), lax.axis_index("col")
    x, z, y, core = col // 4, col % 4, row // 2, row % 2
    width = WIDTH

    def at_x(i):
        return (row, lax.rem(i, 4) * 4 + z)

    def at_z(i):
        return (row, x * 4 + lax.rem(i, 4))

    def at_y(i):
        return (lax.rem(i, 4) * 2 + core, col)

    sibling = (row + 1 - 2 * core, col)
    rings = ((x, z, at_x, at_z), (z, x, at_z, at_x))

    for k in range(steps):
        cols = pl.ds(k * 2 * width, 2 * width)
        pltpu.make_async_copy(wd_hbm.at[cols, :], wd.at[k], w_sem.at[k, 2]).start()
        pltpu.make_async_copy(wg_hbm.at[:, cols], wg.at[k], w_sem.at[k, 0]).start()
        pltpu.make_async_copy(wu_hbm.at[:, cols], wu.at[k], w_sem.at[k, 1]).start()

    own = [
        pltpu.make_async_copy(ref.at[pl.ds(32 * half, 32)], nat.at[a, y, 2 * core + half], tok_sem.at[2 * a + half])
        for a, ref in enumerate((tok_ref, cot_ref))
        for half in range(2)
    ]
    for copy in own:
        copy.start()

    barrier = pltpu.get_barrier_semaphore()
    peers = [at_x(x + 1), at_x(x + 3), at_z(z + 1), at_z(z + 3), at_y(y + 1), at_y(y + 2), at_y(y + 3), sibling]
    for peer in peers:
        pl.semaphore_signal(barrier, inc=1, device_id=peer, device_id_type=MESH)
    pl.semaphore_wait(barrier, len(peers))

    for copy in own:
        copy.wait()

    def rows_of(a, y_at, core_at):
        return nat.at[a, y_at, pl.ds(2 * core_at, 2)]

    def y_copy(a, step, back):
        block = rows_of(a, lax.rem(y + back, 4), core)
        return pltpu.make_async_remote_copy(
            src_ref=block, dst_ref=block, send_sem=g_send.at[a, step], recv_sem=g_recv.at[a, step],
            device_id=at_y(y + step), device_id_type=MESH,
        )

    def core_copy(a, step, core_at):
        block = rows_of(a, lax.rem(y + 4 - step, 4), core_at)
        return pltpu.make_async_remote_copy(
            src_ref=block, dst_ref=block, send_sem=g_send.at[a, 4 + step], recv_sem=g_recv.at[a, 4 + step],
            device_id=sibling, device_id_type=MESH,
        )

    def gathered(a):
        for step in (0, 1, 3, 2):
            core_copy(a, step, 1 - core).wait_recv()
        for i in range(4):
            for j in range(4):
                perm[a, j, i] = nat[a, i, j]

    for a in (1, 0):
        for step in (1, 3, 2):
            y_copy(a, step, 0).start()
        core_copy(a, 0, core).start()
    acc[...] = jnp.zeros_like(acc)
    for a in (1, 0):
        for step in (1, 3, 2):
            y_copy(a, step, 4 - step).wait_recv()
            core_copy(a, step, core).start()
    gathered(1)
    def part(h, k, a, block, first, count):
        tokens = (nat, perm)[h]
        left = tokens[1 if a == 2 else 0, block, pl.ds(first, count)].reshape(count * 32, -1)
        if a == 2:
            return dot_nt(left, wd[k, h * width : (h + 1) * width, :])
        return dot(left, (wg, wu)[a][k, :, h * width : (h + 1) * width])

    def copy_of(kind, k, h, src, dst, target):
        at = 2 * k + h
        return pltpu.make_async_remote_copy(
            src_ref=src, dst_ref=dst, send_sem=send_sem.at[at, kind], recv_sem=recv_sem.at[at, kind],
            device_id=target, device_id_type=MESH,
        )

    def copies(k, h):
        at = 2 * k + h
        p, q, at_p, at_q = rings[h]
        up, down, up2, down2 = at_p(p + 1), at_p(p + 3), at_q(q + 1), at_q(q + 3)
        q_up, q_down = lax.rem(q + 1, 4), lax.rem(q + 3, 4)
        p_up, p_down = lax.rem(p + 1, 4), lax.rem(p + 3, 4)
        table = {}

        def same(kind, src, dst, target):
            table[kind] = (src, dst, target, dst)

        for base, f, fi, n, ni, u, d in (
            (0, far, far_in, near, near_in, up, down),
            (SECOND, far2, far2_in, near2, near2_in, up2, down2),
        ):
            same(base + FAR_UP, f.at[at, 0], fi.at[at, 0], u)
            same(base + FAR_DOWN, f.at[at, 1], fi.at[at, 1], d)
            same(base + SUM_UP, n.at[at, 0, 0], ni.at[at, 0, 0], u)
            same(base + OWN_UP, n.at[at, 0, 1], ni.at[at, 0, 1], u)
            same(base + OWN_DOWN, n.at[at, 1, 0], ni.at[at, 1, 0], d)
            same(base + SUM_DOWN, n.at[at, 1, 1], ni.at[at, 1, 1], d)

        def held(kind, mine, theirs, target):
            table[kind] = (mine, mine, target, theirs)

        mine = all3.at[at, :, p, q]
        held(GIVE_UP, mine, all3.at[at, :, p, q_down], up2)
        held(GIVE_DOWN, mine, all3.at[at, :, p, q_up], down2)
        opp_q, opp_p = lax.rem(q + 2, 4), lax.rem(p + 2, 4)
        low, high = pl.ds(0, 16), pl.ds(16, 16)
        held(PASS_UP, all3.at[at, :, p, q_down, low], all3.at[at, :, p, opp_q, low], up2)
        held(PASS_DOWN, all3.at[at, :, p, q_up, high], all3.at[at, :, p, opp_q, high], down2)
        held(WIDE_UP, all3.at[at, :, p], all3.at[at, :, p_down], up)
        held(WIDE_DOWN, all3.at[at, :, p], all3.at[at, :, p_up], down)
        low, high = pl.ds(0, 2), pl.ds(2, 2)
        held(WIDE_PASS_UP, all3.at[at, :, p_down, low], all3.at[at, :, opp_p, low], up)
        held(WIDE_PASS_DOWN, all3.at[at, :, p_up, high], all3.at[at, :, opp_p, high], down)
        return table

    def start(k, h, *kinds, arrays=None):
        table = copies(k, h)
        for kind in kinds:
            src, dst, target, _ = table[kind]
            if arrays is not None:
                src, dst = src.at[arrays], dst.at[arrays]
            copy_of(kind, k, h, src, dst, target).start()

    def arrive(k, h, *kinds):
        table = copies(k, h)
        for kind in kinds:
            src, _, target, here = table[kind]
            copy_of(kind, k, h, here, here, target).wait_recv()

    def sent(k, h):
        for kind, (src, dst, target, _) in copies(k, h).items():
            copy_of(kind, k, h, src, dst, target).wait_send()

    def first_sums(k, h, a):
        p = rings[h][0]
        at = 2 * k + h
        whole = part(h, k, a, lax.rem(p + 2, 4), 0, 4).astype(BF16)
        far[at, 0, a] = whole[:64]
        far[at, 1, a] = whole[64:]
        near[at, 0, 1, a] = part(h, k, a, lax.rem(p + 1, 4), 2, 2).astype(BF16)
        near[at, 1, 0, a] = part(h, k, a, lax.rem(p + 3, 4), 0, 2).astype(BF16)

    firsts = (FAR_UP, FAR_DOWN, OWN_UP, OWN_DOWN)

    def hidden_grad_sums(k):
        cols = pl.ds(0, 2 * width)
        pltpu.make_async_copy(wd_hbm.at[cols, :], wd.at[k], w_sem.at[k, 2]).wait()
        for h in range(2):
            first_sums(k, h, 2)

    def stage0(k):
        cols = pl.ds(0, 2 * width)

        @pl.when(k == 0)
        def _():
            for ahead in range(AHEAD):
                hidden_grad_sums(ahead)
                for h in range(2):
                    start(ahead, h, *firsts, arrays=pl.ds(2, 1))
            gathered(0)

        @pl.when(k >= AHEAD)
        def _():
            hidden_grad_sums(k)

        pltpu.make_async_copy(wg_hbm.at[:, cols], wg.at[k], w_sem.at[k, 0]).wait()
        pltpu.make_async_copy(wu_hbm.at[:, cols], wu.at[k], w_sem.at[k, 1]).wait()
        for h in range(2):
            for a in range(2):
                first_sums(k, h, a)

            @pl.when(k < AHEAD)
            def _():
                start(k, h, *firsts, arrays=pl.ds(0, 2))

            @pl.when(k >= AHEAD)
            def _():
                start(k, h, *firsts)

        @pl.when(k == 0)
        def _():
            for h, tokens in enumerate((nat, perm)):
                tok_t[h] = tokens[0].reshape(tok_t.shape[1:]).T

    def stage1(k):
        for h in range(2):
            p = rings[h][0]
            at = 2 * k + h
            arrive(k, h, FAR_UP, FAR_DOWN)
            for a in range(3):
                near[at, 0, 0, a] = (
                    part(h, k, a, lax.rem(p + 1, 4), 0, 2) + far_in[at, 0, a].astype(F32)
                ).astype(BF16)
                near[at, 1, 1, a] = (
                    part(h, k, a, lax.rem(p + 3, 4), 2, 2) + far_in[at, 1, a].astype(F32)
                ).astype(BF16)
            start(k, h, SUM_UP, SUM_DOWN)

    def stage2(k):
        slot = lax.rem(k, 3)
        for h in range(2):
            p, q = rings[h][:2]
            at = 2 * k + h
            arrive(k, h, OWN_UP, OWN_DOWN, SUM_UP, SUM_DOWN)
            for a in range(3):
                for half in range(2):
                    total = (
                        part(h, k, a, p, 2 * half, 2)
                        + near_in[at, 0, half, a].astype(F32)
                        + near_in[at, 1, half, a].astype(F32)
                    )
                    sub[slot, h, a, 2 * half] = total[:32]
                    sub[slot, h, a, 2 * half + 1] = total[32:]
            for a in range(3):
                opposite = sub[slot, h, a, lax.rem(q + 2, 4)].astype(BF16)
                far2[at, 0, a] = opposite[:16]
                far2[at, 1, a] = opposite[16:]
                near2[at, 0, 1, a] = sub[slot, h, a, lax.rem(q + 1, 4), 16:, :].astype(BF16)
                near2[at, 1, 0, a] = sub[slot, h, a, lax.rem(q + 3, 4), :16, :].astype(BF16)
            start(k, h, *(SECOND + kind for kind in (FAR_UP, FAR_DOWN, OWN_UP, OWN_DOWN)))

    def stage3(k):
        slot = lax.rem(k, 3)
        for h in range(2):
            q = rings[h][1]
            at = 2 * k + h
            arrive(k, h, SECOND + FAR_UP, SECOND + FAR_DOWN)
            for a in range(3):
                near2[at, 0, 0, a] = (
                    sub[slot, h, a, lax.rem(q + 1, 4), :16, :] + far2_in[at, 0, a].astype(F32)
                ).astype(BF16)
                near2[at, 1, 1, a] = (
                    sub[slot, h, a, lax.rem(q + 3, 4), 16:, :] + far2_in[at, 1, a].astype(F32)
                ).astype(BF16)
            start(k, h, SECOND + SUM_UP, SECOND + SUM_DOWN)

    def stage4(k):
        slot = lax.rem(k, 3)
        for h in range(2):
            p, q = rings[h][:2]
            at = 2 * k + h
            arrive(k, h, *(SECOND + kind for kind in (OWN_UP, OWN_DOWN, SUM_UP, SUM_DOWN)))
            for half in range(2):
                rows = slice(16 * half, 16 * half + 16)
                gate, up, hidden_grad = (
                    sub[slot, h, a, q, rows, :]
                    + near2_in[at, 0, half, a].astype(F32)
                    + near2_in[at, 1, half, a].astype(F32)
                    for a in range(3)
                )
                sigmoid_gate = 1.0 / (1.0 + jnp.exp(-gate))
                activated = gate * sigmoid_gate
                all3[at, 0, p, q, rows, :] = (activated * up).astype(BF16)
                all3[at, 1, p, q, rows, :] = (
                    hidden_grad * up * sigmoid_gate * (1.0 + gate * (1.0 - sigmoid_gate))
                ).astype(BF16)
                all3[at, 2, p, q, rows, :] = (hidden_grad * activated).astype(BF16)
            start(k, h, GIVE_UP, GIVE_DOWN)

    def stage5(k):
        for h in range(2):
            arrive(k, h, GIVE_UP, GIVE_DOWN)
            start(k, h, PASS_UP, PASS_DOWN)

    def stage6(k):
        for h in range(2):
            arrive(k, h, PASS_UP, PASS_DOWN)
            start(k, h, WIDE_UP, WIDE_DOWN)

    def stage7(k):
        for h in range(2):
            arrive(k, h, WIDE_UP, WIDE_DOWN)
            start(k, h, WIDE_PASS_UP, WIDE_PASS_DOWN)

    def grad_copies(k):
        slot = lax.rem(k, 2)
        copies_out = []
        for h in range(2):
            span = pl.ds(pl.multiple_of((2 * k + h) * width, width), width)
            for a, (out, src) in enumerate(
                ((gg_out.at[:, span], grads.at[slot, h, 0]), (ug_out.at[:, span], grads.at[slot, h, 1]),
                 (dg_out.at[span, :], down_grads.at[slot, h]))
            ):
                copies_out.append(pltpu.make_async_copy(src, out, out_sem.at[k, h, a]))
        return copies_out

    def stage9(k):
        slot = lax.rem(k, 2)

        @pl.when(k >= 2)
        def _():
            for copy in grad_copies(k - 2):
                copy.wait()

        for h in range(2):
            at = 2 * k + h
            for a in range(2):
                grads[slot, h, a] = dot(tok_t[h], all3[at, 1 + a].reshape(512, width)).astype(BF16)
            cot_all = (nat, perm)[h][1].reshape(512, -1)
            down_grads[slot, h] = dot_tn(all3[at, 0].reshape(512, width), cot_all).astype(BF16)
        for copy in grad_copies(k):
            copy.start()

    def stage8(k):
        late = (k >= EARLY).astype(jnp.int32)
        for h in range(2):
            arrive(k, h, WIDE_PASS_UP, WIDE_PASS_DOWN)
        for h in range(2):
            at = 2 * k + h
            sent(k, h)
            hidden_rows = slice(h * width, (h + 1) * width)
            for b in range(4):
                hidden, gate_grad, up_grad = (all3[at, a, b].reshape(128, width) for a in range(3))
                mixed = dot(hidden, wd[k, hidden_rows, :])
                into = dot_nt(gate_grad, wg[k, :, hidden_rows]) + dot_nt(up_grad, wu[k, :, hidden_rows])
                for j in range(4):
                    rows = slice(32 * j, 32 * j + 32)
                    i, jj = (b, j) if h == 0 else (j, b)
                    acc[late, 0, i, jj] += mixed[rows]
                    acc[late, 1, i, jj] += into[rows]

    order = (2, 1, 3, 0)

    def core_sum(late, step):
        block = acc.at[late, :, lax.rem(y + step, 4), pl.ds(2 * (1 - core), 2)]
        return pltpu.make_async_remote_copy(
            src_ref=block, dst_ref=core_in.at[late, step], send_sem=r_send.at[late, step],
            recv_sem=r_recv.at[late, step], device_id=sibling, device_id_type=MESH,
        )

    def chip_sum(late, step):
        core_sum(late, step).wait_recv()
        return acc[late, :, lax.rem(y + step, 4), pl.ds(2 * core, 2)] + core_in[late, step]

    def y_sum(step):
        return pltpu.make_async_remote_copy(
            src_ref=y_send.at[step], dst_ref=y_in.at[step], send_sem=y_sem.at[0, step], recv_sem=y_sem.at[1, step],
            device_id=at_y(y + step), device_id_type=MESH,
        )

    stages = (stage0, stage1, stage2, stage3, stage4, stage5, stage6, stage7, stage8, stage9)

    def turn(i, carry):
        for late, stage in enumerate(stages):
            @pl.when((i >= late) & (i < steps + late))
            def _():
                stage(i - late)

            if late == 8:
                @pl.when(i == EARLY + DEPTH - 1)
                def _():
                    for step in order:
                        core_sum(0, step).start()

            if late == 9:
                @pl.when(i == EARLY + DEPTH - 1)
                def _():
                    for step in order:
                        y_send[step] = chip_sum(0, step)
                        if step:
                            y_sum(step).start()

        return carry

    lax.fori_loop(0, steps + DEPTH, turn, 0)

    for step in order:
        core_sum(1, step).start()
    stage9(steps - 1)
    for step in order[:3]:
        total = chip_sum(1, step)
        for j in range(2):
            sum_outs[step][:, 32 * j : 32 * j + 32, :] = total[:, j].astype(BF16)
    total = chip_sum(1, 0) + y_send[0]
    for step in (1, 3, 2):
        y_sum(step).wait_recv()
        total += y_in[step]
    for j in range(2):
        own_out[:, 32 * j : 32 * j + 32, :] = total[:, j]
    for step in order:
        for late in range(2):
            core_sum(late, step).wait_send()
        if step:
            y_sum(step).wait_send()
    for a in range(2):
        for step in (1, 2, 3):
            y_copy(a, step, 0).wait_send()
        for step in range(4):
            core_copy(a, step, core).wait_send()

    for k in (steps - 2, steps - 1):
        for copy in grad_copies(k):
            copy.wait()


def ring_call(tokens, w_gate, w_up, w_down, cotangent):
    features, hidden = w_gate.shape
    steps = hidden // (2 * WIDTH)
    parts = 2 * steps
    any_space = pl.BlockSpec(memory_space=pl.ANY)
    vmem = pl.BlockSpec(memory_space=pltpu.VMEM)

    def kernel(*refs):
        ring_kernel(steps, *refs)

    wide = jax.ShapeDtypeStruct((features, hidden), BF16)
    tall = jax.ShapeDtypeStruct((hidden, features), BF16)
    dma = pltpu.SemaphoreType.DMA
    return pl.pallas_call(
        kernel,
        out_shape=(wide, wide, tall) + (jax.ShapeDtypeStruct((2, 64, features), F32),)
        + (jax.ShapeDtypeStruct((2, 64, features), BF16),) * 3,
        in_specs=[any_space] * 5,
        out_specs=(any_space,) * 3 + (vmem,) * 4,
        scratch_shapes=[
            pltpu.VMEM((steps, features, 2 * WIDTH), BF16),
            pltpu.VMEM((steps, features, 2 * WIDTH), BF16),
            pltpu.VMEM((steps, 2 * WIDTH, features), BF16),
            pltpu.VMEM((2, 4, 4, 32, features), BF16),
            pltpu.VMEM((2, 4, 4, 32, features), BF16),
            pltpu.VMEM((parts, 2, 3, 64, WIDTH), BF16),
            pltpu.VMEM((parts, 2, 3, 64, WIDTH), BF16),
            pltpu.VMEM((parts, 2, 2, 3, 64, WIDTH), BF16),
            pltpu.VMEM((parts, 2, 2, 3, 64, WIDTH), BF16),
            pltpu.VMEM((parts, 2, 3, 16, WIDTH), BF16),
            pltpu.VMEM((parts, 2, 3, 16, WIDTH), BF16),
            pltpu.VMEM((parts, 2, 2, 3, 16, WIDTH), BF16),
            pltpu.VMEM((parts, 2, 2, 3, 16, WIDTH), BF16),
            pltpu.VMEM((3, 2, 3, 4, 32, WIDTH), F32),
            pltpu.VMEM((parts, 3, 4, 4, 32, WIDTH), BF16),
            pltpu.VMEM((2, features, 512), BF16),
            pltpu.VMEM((2, 2, 2, features, WIDTH), BF16),
            pltpu.VMEM((2, 2, WIDTH, features), BF16),
            pltpu.VMEM((2, 2, 4, 4, 32, features), F32),
            pltpu.VMEM((2, 4, 2, 2, 32, features), F32),
            pltpu.VMEM((4, 2, 2, 32, features), F32),
            pltpu.VMEM((4, 2, 2, 32, features), F32),
            dma((parts, COPIES)),
            dma((parts, COPIES)),
            dma((steps, 3)),
            dma((steps, 2, 3)),
            dma((2, 8)),
            dma((2, 8)),
            dma((2, 4)),
            dma((2, 4)),
            dma((2, 4)),
            dma((4,)),
        ],
        name="ring_sums",
        compiler_params=pltpu.CompilerParams(
            collective_id=0, has_side_effects=True, vmem_limit_bytes=62 * 2**20
        ),
    )(tokens, cotangent, w_gate, w_up, w_down)


def along_y(block, step):
    rows = lax.axis_size("row")
    return lax.ppermute(block, "row", [(r, (r + 2 * step) % rows) for r in range(rows)])


def keep_kernel(*refs):
    for src, dst in zip(refs[:3], refs[3:]):
        dst[...] = src[...]


def keep(*arrays):
    specs = [pl.BlockSpec((a.shape[0] // KEEP_PARTS, a.shape[1]), lambda i: (i, 0)) for a in arrays]
    return pl.pallas_call(
        keep_kernel,
        out_shape=tuple(jax.ShapeDtypeStruct(a.shape, a.dtype) for a in arrays),
        grid=(KEEP_PARTS,),
        in_specs=specs,
        out_specs=tuple(specs),
        name="keep",
        compiler_params=pltpu.CompilerParams(vmem_limit_bytes=62 * 2**20),
        cost_estimate=pl.CostEstimate(flops=0, transcendentals=0, bytes_accessed=sum(4 * a.size for a in arrays)),
    )(*arrays)


def shards(tokens, w_gate, w_up, w_down, cotangent):
    gate_wgrad, up_wgrad, down_wgrad, own, *sums = ring_call(tokens, w_gate, w_up, w_down, cotangent)
    came = [along_y(block, step + 1) for step, block in enumerate(sums)]
    weight_grads = keep(gate_wgrad, up_wgrad, down_wgrad)
    mixed, input_grad = (
        (own[i] + came[0][i].astype(F32) + came[1][i].astype(F32) + came[2][i].astype(F32)).astype(BF16)
        for i in range(2)
    )
    return (mixed, input_grad, *weight_grads)


def solution(mesh):
    return jax.shard_map(
        shards,
        mesh=mesh,
        in_specs=(P("row", "col"), P("col", "row"), P("col", "row"), P("row", "col"), P("row", "col")),
        out_specs=(P("row", "col"), P("row", "col"), P("col", "row"), P("col", "row"), P("row", "col")),
        check_vma=False,
    )
```

```python
import jax
import jax.numpy as jnp
from jax import lax
from jax.experimental import pallas as pl
from jax.experimental.pallas import tpu as pltpu
from jax.sharding import PartitionSpec as P

MESH = pl.DeviceIdType.MESH
BF16 = jnp.bfloat16
F32 = jnp.float32
WIDTH = 256
DEPTH = 8
EARLY = 4
AHEAD = 2
KEEP_PARTS = 2

FAR_UP, FAR_DOWN, OWN_UP, OWN_DOWN, SUM_UP, SUM_DOWN = range(6)
SECOND = 6
GIVE_UP, GIVE_DOWN, PASS_UP, PASS_DOWN = range(12, 16)
WIDE_UP, WIDE_DOWN, WIDE_PASS_UP, WIDE_PASS_DOWN = range(16, 20)
COPIES = 20


def dot(left, right):
    return jnp.dot(left, right, preferred_element_type=F32)


def dot_nt(left, right):
    return lax.dot_general(left, right, (((1,), (1,)), ((), ())), preferred_element_type=F32)


def dot_tn(left, right):
    return lax.dot_general(left, right, (((0,), (0,)), ((), ())), preferred_element_type=F32)


def ring_kernel(
    steps,
    tok_ref, cot_ref, wg_hbm, wu_hbm, wd_hbm,
    gg_out, ug_out, dg_out, own_out, sum1, sum2, sum3,
    wg, wu, wd, nat, perm, far, far_in, near, near_in,
    far2, far2_in, near2, near2_in, sub, all3, tok_t, grads, down_grads, acc, core_in, y_send, y_in,
    send_sem, recv_sem, w_sem, out_sem, g_send, g_recv, r_send, r_recv, y_sem, tok_sem,
):
    sum_outs = (own_out, sum1, sum2, sum3)
    row, col = lax.axis_index("row"), lax.axis_index("col")
    x, z, y, core = col // 4, col % 4, row // 2, row % 2
    width = WIDTH

    def at_x(i):
        return (row, lax.rem(i, 4) * 4 + z)

    def at_z(i):
        return (row, x * 4 + lax.rem(i, 4))

    def at_y(i):
        return (lax.rem(i, 4) * 2 + core, col)

    sibling = (row + 1 - 2 * core, col)
    rings = ((x, z, at_x, at_z), (z, x, at_z, at_x))

    own = [
        pltpu.make_async_copy(ref.at[pl.ds(32 * half, 32)], nat.at[a, y, 2 * core + half], tok_sem.at[2 * a + half])
        for a, ref in enumerate((tok_ref, cot_ref))
        for half in range(2)
    ]
    for copy in own:
        copy.start()

    barrier = pltpu.get_barrier_semaphore()
    peers = [at_x(x + 1), at_x(x + 3), at_z(z + 1), at_z(z + 3), at_y(y + 1), at_y(y + 2), at_y(y + 3), sibling]
    for peer in peers:
        pl.semaphore_signal(barrier, inc=1, device_id=peer, device_id_type=MESH)
    def fetch(k):
        cols = pl.ds(k * 2 * width, 2 * width)
        pltpu.make_async_copy(wd_hbm.at[cols, :], wd.at[k], w_sem.at[k, 2]).start()
        pltpu.make_async_copy(wg_hbm.at[:, cols], wg.at[k], w_sem.at[k, 0]).start()
        pltpu.make_async_copy(wu_hbm.at[:, cols], wu.at[k], w_sem.at[k, 1]).start()

    fetch(0)
    acc[...] = jnp.zeros_like(acc)
    pl.semaphore_wait(barrier, len(peers))

    for copy in own:
        copy.wait()

    def rows_of(a, y_at, core_at):
        return nat.at[a, y_at, pl.ds(2 * core_at, 2)]

    def y_copy(a, step, back):
        block = rows_of(a, lax.rem(y + back, 4), core)
        return pltpu.make_async_remote_copy(
            src_ref=block, dst_ref=block, send_sem=g_send.at[a, step], recv_sem=g_recv.at[a, step],
            device_id=at_y(y + step), device_id_type=MESH,
        )

    def core_copy(a, step, core_at):
        block = rows_of(a, lax.rem(y + 4 - step, 4), core_at)
        return pltpu.make_async_remote_copy(
            src_ref=block, dst_ref=block, send_sem=g_send.at[a, 4 + step], recv_sem=g_recv.at[a, 4 + step],
            device_id=sibling, device_id_type=MESH,
        )

    def gathered(a):
        for step in (0, 1, 3, 2):
            core_copy(a, step, 1 - core).wait_recv()
        for i in range(4):
            for j in range(4):
                perm[a, j, i] = nat[a, i, j]

    for a in (1, 0):
        for step in (1, 3, 2):
            y_copy(a, step, 0).start()
        core_copy(a, 0, core).start()
    for k in range(1, steps):
        fetch(k)

    def along_core(a):
        for step in (1, 3, 2):
            y_copy(a, step, 4 - step).wait_recv()
            core_copy(a, step, core).start()

    along_core(1)
    gathered(1)
    def part(h, k, a, block, first, count):
        tokens = (nat, perm)[h]
        left = tokens[1 if a == 2 else 0, block, pl.ds(first, count)].reshape(count * 32, -1)
        if a == 2:
            return dot_nt(left, wd[k, h * width : (h + 1) * width, :])
        return dot(left, (wg, wu)[a][k, :, h * width : (h + 1) * width])

    def copy_of(kind, k, h, src, dst, target):
        at = 2 * k + h
        return pltpu.make_async_remote_copy(
            src_ref=src, dst_ref=dst, send_sem=send_sem.at[at, kind], recv_sem=recv_sem.at[at, kind],
            device_id=target, device_id_type=MESH,
        )

    def copies(k, h):
        at = 2 * k + h
        p, q, at_p, at_q = rings[h]
        up, down, up2, down2 = at_p(p + 1), at_p(p + 3), at_q(q + 1), at_q(q + 3)
        q_up, q_down = lax.rem(q + 1, 4), lax.rem(q + 3, 4)
        p_up, p_down = lax.rem(p + 1, 4), lax.rem(p + 3, 4)
        table = {}

        def same(kind, src, dst, target):
            table[kind] = (src, dst, target, dst)

        for base, f, fi, n, ni, u, d in (
            (0, far, far_in, near, near_in, up, down),
            (SECOND, far2, far2_in, near2, near2_in, up2, down2),
        ):
            same(base + FAR_UP, f.at[at, 0], fi.at[at, 0], u)
            same(base + FAR_DOWN, f.at[at, 1], fi.at[at, 1], d)
            same(base + SUM_UP, n.at[at, 0, 0], ni.at[at, 0, 0], u)
            same(base + OWN_UP, n.at[at, 0, 1], ni.at[at, 0, 1], u)
            same(base + OWN_DOWN, n.at[at, 1, 0], ni.at[at, 1, 0], d)
            same(base + SUM_DOWN, n.at[at, 1, 1], ni.at[at, 1, 1], d)

        def held(kind, mine, theirs, target):
            table[kind] = (mine, mine, target, theirs)

        mine = all3.at[at, :, p, q]
        held(GIVE_UP, mine, all3.at[at, :, p, q_down], up2)
        held(GIVE_DOWN, mine, all3.at[at, :, p, q_up], down2)
        opp_q, opp_p = lax.rem(q + 2, 4), lax.rem(p + 2, 4)
        low, high = pl.ds(0, 16), pl.ds(16, 16)
        held(PASS_UP, all3.at[at, :, p, q_down, low], all3.at[at, :, p, opp_q, low], up2)
        held(PASS_DOWN, all3.at[at, :, p, q_up, high], all3.at[at, :, p, opp_q, high], down2)
        held(WIDE_UP, all3.at[at, :, p], all3.at[at, :, p_down], up)
        held(WIDE_DOWN, all3.at[at, :, p], all3.at[at, :, p_up], down)
        low, high = pl.ds(0, 2), pl.ds(2, 2)
        held(WIDE_PASS_UP, all3.at[at, :, p_down, low], all3.at[at, :, opp_p, low], up)
        held(WIDE_PASS_DOWN, all3.at[at, :, p_up, high], all3.at[at, :, opp_p, high], down)
        return table

    def start(k, h, *kinds, arrays=None):
        table = copies(k, h)
        for kind in kinds:
            src, dst, target, _ = table[kind]
            if arrays is not None:
                src, dst = src.at[arrays], dst.at[arrays]
            copy_of(kind, k, h, src, dst, target).start()

    def arrive(k, h, *kinds):
        table = copies(k, h)
        for kind in kinds:
            src, _, target, here = table[kind]
            copy_of(kind, k, h, here, here, target).wait_recv()

    def sent(k, h):
        for kind, (src, dst, target, _) in copies(k, h).items():
            copy_of(kind, k, h, src, dst, target).wait_send()

    def first_sums(k, h, a):
        p = rings[h][0]
        at = 2 * k + h
        whole = part(h, k, a, lax.rem(p + 2, 4), 0, 4).astype(BF16)
        far[at, 0, a] = whole[:64]
        far[at, 1, a] = whole[64:]
        near[at, 0, 1, a] = part(h, k, a, lax.rem(p + 1, 4), 2, 2).astype(BF16)
        near[at, 1, 0, a] = part(h, k, a, lax.rem(p + 3, 4), 0, 2).astype(BF16)

    firsts = (FAR_UP, FAR_DOWN, OWN_UP, OWN_DOWN)

    def hidden_grad_sums(k, send):
        cols = pl.ds(0, 2 * width)
        pltpu.make_async_copy(wd_hbm.at[cols, :], wd.at[k], w_sem.at[k, 2]).wait()
        for h in range(2):
            first_sums(k, h, 2)
            if send:
                start(k, h, *firsts, arrays=pl.ds(2, 1))

    def stage0(k):
        cols = pl.ds(0, 2 * width)

        @pl.when(k == 0)
        def _():
            for ahead in range(AHEAD):
                hidden_grad_sums(ahead, True)
                if ahead == 0:
                    along_core(0)
            gathered(0)

        @pl.when(k >= AHEAD)
        def _():
            hidden_grad_sums(k, False)

        pltpu.make_async_copy(wg_hbm.at[:, cols], wg.at[k], w_sem.at[k, 0]).wait()
        pltpu.make_async_copy(wu_hbm.at[:, cols], wu.at[k], w_sem.at[k, 1]).wait()
        for h in range(2):
            for a in range(2):
                first_sums(k, h, a)

            @pl.when(k < AHEAD)
            def _():
                start(k, h, *firsts, arrays=pl.ds(0, 2))

            @pl.when(k >= AHEAD)
            def _():
                start(k, h, *firsts)

        @pl.when(k == 3)
        def _():
            for h, tokens in enumerate((nat, perm)):
                tok_t[h] = tokens[0].reshape(tok_t.shape[1:]).T

    def stage1(k):
        for h in range(2):
            p = rings[h][0]
            at = 2 * k + h
            arrive(k, h, FAR_UP, FAR_DOWN)
            for a in range(3):
                near[at, 0, 0, a] = (
                    part(h, k, a, lax.rem(p + 1, 4), 0, 2) + far_in[at, 0, a].astype(F32)
                ).astype(BF16)
                near[at, 1, 1, a] = (
                    part(h, k, a, lax.rem(p + 3, 4), 2, 2) + far_in[at, 1, a].astype(F32)
                ).astype(BF16)
            start(k, h, SUM_UP, SUM_DOWN)

    def stage2(k):
        slot = lax.rem(k, 3)
        for h in range(2):
            p, q = rings[h][:2]
            at = 2 * k + h
            arrive(k, h, OWN_UP, OWN_DOWN, SUM_UP, SUM_DOWN)
            for a in range(3):
                for half in range(2):
                    total = (
                        part(h, k, a, p, 2 * half, 2)
                        + near_in[at, 0, half, a].astype(F32)
                        + near_in[at, 1, half, a].astype(F32)
                    )
                    sub[slot, h, a, 2 * half] = total[:32]
                    sub[slot, h, a, 2 * half + 1] = total[32:]
            for a in range(3):
                opposite = sub[slot, h, a, lax.rem(q + 2, 4)].astype(BF16)
                far2[at, 0, a] = opposite[:16]
                far2[at, 1, a] = opposite[16:]
                near2[at, 0, 1, a] = sub[slot, h, a, lax.rem(q + 1, 4), 16:, :].astype(BF16)
                near2[at, 1, 0, a] = sub[slot, h, a, lax.rem(q + 3, 4), :16, :].astype(BF16)
            start(k, h, *(SECOND + kind for kind in (FAR_UP, FAR_DOWN, OWN_UP, OWN_DOWN)))

    def stage3(k):
        slot = lax.rem(k, 3)
        for h in range(2):
            q = rings[h][1]
            at = 2 * k + h
            arrive(k, h, SECOND + FAR_UP, SECOND + FAR_DOWN)
            for a in range(3):
                near2[at, 0, 0, a] = (
                    sub[slot, h, a, lax.rem(q + 1, 4), :16, :] + far2_in[at, 0, a].astype(F32)
                ).astype(BF16)
                near2[at, 1, 1, a] = (
                    sub[slot, h, a, lax.rem(q + 3, 4), 16:, :] + far2_in[at, 1, a].astype(F32)
                ).astype(BF16)
            start(k, h, SECOND + SUM_UP, SECOND + SUM_DOWN)

    def stage4(k):
        slot = lax.rem(k, 3)
        for h in range(2):
            p, q = rings[h][:2]
            at = 2 * k + h
            arrive(k, h, *(SECOND + kind for kind in (OWN_UP, OWN_DOWN, SUM_UP, SUM_DOWN)))
            for half in range(2):
                rows = slice(16 * half, 16 * half + 16)
                gate, up, hidden_grad = (
                    sub[slot, h, a, q, rows, :]
                    + near2_in[at, 0, half, a].astype(F32)
                    + near2_in[at, 1, half, a].astype(F32)
                    for a in range(3)
                )
                sigmoid_gate = 1.0 / (1.0 + jnp.exp(-gate))
                activated = gate * sigmoid_gate
                all3[at, 0, p, q, rows, :] = (activated * up).astype(BF16)
                all3[at, 1, p, q, rows, :] = (
                    hidden_grad * up * sigmoid_gate * (1.0 + gate * (1.0 - sigmoid_gate))
                ).astype(BF16)
                all3[at, 2, p, q, rows, :] = (hidden_grad * activated).astype(BF16)
            start(k, h, GIVE_UP, GIVE_DOWN)

    def stage5(k):
        for h in range(2):
            arrive(k, h, GIVE_UP, GIVE_DOWN)
            start(k, h, PASS_UP, PASS_DOWN)

    def stage6(k):
        for h in range(2):
            arrive(k, h, PASS_UP, PASS_DOWN)
            start(k, h, WIDE_UP, WIDE_DOWN)

    def stage7(k):
        for h in range(2):
            arrive(k, h, WIDE_UP, WIDE_DOWN)
            start(k, h, WIDE_PASS_UP, WIDE_PASS_DOWN)

    def grad_copies(k):
        slot = lax.rem(k, 2)
        copies_out = []
        for h in range(2):
            span = pl.ds(pl.multiple_of((2 * k + h) * width, width), width)
            for a, (out, src) in enumerate(
                ((gg_out.at[:, span], grads.at[slot, h, 0]), (ug_out.at[:, span], grads.at[slot, h, 1]),
                 (dg_out.at[span, :], down_grads.at[slot, h]))
            ):
                copies_out.append(pltpu.make_async_copy(src, out, out_sem.at[k, h, a]))
        return copies_out

    def stage9(k):
        slot = lax.rem(k, 2)

        @pl.when(k >= 2)
        def _():
            for copy in grad_copies(k - 2):
                copy.wait()

        for h in range(2):
            at = 2 * k + h
            sent(k, h)
            for a in range(2):
                grads[slot, h, a] = dot(tok_t[h], all3[at, 1 + a].reshape(512, width)).astype(BF16)
            cot_all = (nat, perm)[h][1].reshape(512, -1)
            down_grads[slot, h] = dot_tn(all3[at, 0].reshape(512, width), cot_all).astype(BF16)
        for copy in grad_copies(k):
            copy.start()

    def stage8(k):
        late = (k >= EARLY).astype(jnp.int32)
        for last in range(2):
            for h in range(2):
                at = 2 * k + h
                if last:
                    arrive(k, h, WIDE_PASS_UP, WIDE_PASS_DOWN)
                hidden_rows = slice(h * width, (h + 1) * width)
                for ahead in (2,) if last else (0, 1, 3):
                    b = lax.rem(rings[h][0] + ahead, 4)
                    hidden, gate_grad, up_grad = (all3[at, a, b].reshape(128, width) for a in range(3))
                    mixed = dot(hidden, wd[k, hidden_rows, :])
                    into = dot_nt(gate_grad, wg[k, :, hidden_rows]) + dot_nt(up_grad, wu[k, :, hidden_rows])
                    for j in range(4):
                        rows = slice(32 * j, 32 * j + 32)
                        i, jj = (b, j) if h == 0 else (j, b)
                        acc[late, 0, i, jj] += mixed[rows]
                        acc[late, 1, i, jj] += into[rows]

    order = (2, 1, 3, 0)

    def core_sum(late, step):
        block = acc.at[late, :, lax.rem(y + step, 4), pl.ds(2 * (1 - core), 2)]
        return pltpu.make_async_remote_copy(
            src_ref=block, dst_ref=core_in.at[late, step], send_sem=r_send.at[late, step],
            recv_sem=r_recv.at[late, step], device_id=sibling, device_id_type=MESH,
        )

    def chip_sum(late, step):
        core_sum(late, step).wait_recv()
        return acc[late, :, lax.rem(y + step, 4), pl.ds(2 * core, 2)] + core_in[late, step]

    def y_sum(step):
        return pltpu.make_async_remote_copy(
            src_ref=y_send.at[step], dst_ref=y_in.at[step], send_sem=y_sem.at[0, step], recv_sem=y_sem.at[1, step],
            device_id=at_y(y + step), device_id_type=MESH,
        )

    stages = (stage0, stage1, stage2, stage3, stage4, stage5, stage6, stage7, stage8)

    def turn(i, carry):
        for late, stage in enumerate(stages):
            @pl.when((i >= late) & (i < steps + late))
            def _():
                stage(i - late)

        @pl.when(i == EARLY + DEPTH - 1)
        def _():
            for step in order:
                core_sum(0, step).start()

        @pl.when(i == steps + DEPTH - 1)
        def _():
            for step in order:
                core_sum(1, step).start()

        @pl.when(i >= DEPTH)
        def _():
            stage9(i - DEPTH)

        @pl.when(i == EARLY + DEPTH - 1)
        def _():
            for step in order:
                y_send[step] = chip_sum(0, step)
                if step:
                    y_sum(step).start()
        return carry

    lax.fori_loop(0, steps + DEPTH, turn, 0)

    for step in order[:3]:
        total = chip_sum(1, step)
        for j in range(2):
            sum_outs[step][:, 32 * j : 32 * j + 32, :] = total[:, j].astype(BF16)
    total = chip_sum(1, 0) + y_send[0]
    for step in (1, 3, 2):
        y_sum(step).wait_recv()
        total += y_in[step]
    for j in range(2):
        own_out[:, 32 * j : 32 * j + 32, :] = total[:, j]
    for step in order:
        for late in range(2):
            core_sum(late, step).wait_send()
        if step:
            y_sum(step).wait_send()
    for a in range(2):
        for step in (1, 2, 3):
            y_copy(a, step, 0).wait_send()
        for step in range(4):
            core_copy(a, step, core).wait_send()

    for k in (steps - 2, steps - 1):
        for copy in grad_copies(k):
            copy.wait()


def ring_call(tokens, w_gate, w_up, w_down, cotangent):
    features, hidden = w_gate.shape
    steps = hidden // (2 * WIDTH)
    parts = 2 * steps
    any_space = pl.BlockSpec(memory_space=pl.ANY)
    vmem = pl.BlockSpec(memory_space=pltpu.VMEM)

    def kernel(*refs):
        ring_kernel(steps, *refs)

    wide = jax.ShapeDtypeStruct((features, hidden), BF16)
    tall = jax.ShapeDtypeStruct((hidden, features), BF16)
    dma = pltpu.SemaphoreType.DMA
    return pl.pallas_call(
        kernel,
        out_shape=(wide, wide, tall) + (jax.ShapeDtypeStruct((2, 64, features), F32),)
        + (jax.ShapeDtypeStruct((2, 64, features), BF16),) * 3,
        in_specs=[any_space] * 5,
        out_specs=(any_space,) * 3 + (vmem,) * 4,
        scratch_shapes=[
            pltpu.VMEM((steps, features, 2 * WIDTH), BF16),
            pltpu.VMEM((steps, features, 2 * WIDTH), BF16),
            pltpu.VMEM((steps, 2 * WIDTH, features), BF16),
            pltpu.VMEM((2, 4, 4, 32, features), BF16),
            pltpu.VMEM((2, 4, 4, 32, features), BF16),
            pltpu.VMEM((parts, 2, 3, 64, WIDTH), BF16),
            pltpu.VMEM((parts, 2, 3, 64, WIDTH), BF16),
            pltpu.VMEM((parts, 2, 2, 3, 64, WIDTH), BF16),
            pltpu.VMEM((parts, 2, 2, 3, 64, WIDTH), BF16),
            pltpu.VMEM((parts, 2, 3, 16, WIDTH), BF16),
            pltpu.VMEM((parts, 2, 3, 16, WIDTH), BF16),
            pltpu.VMEM((parts, 2, 2, 3, 16, WIDTH), BF16),
            pltpu.VMEM((parts, 2, 2, 3, 16, WIDTH), BF16),
            pltpu.VMEM((3, 2, 3, 4, 32, WIDTH), F32),
            pltpu.VMEM((parts, 3, 4, 4, 32, WIDTH), BF16),
            pltpu.VMEM((2, features, 512), BF16),
            pltpu.VMEM((2, 2, 2, features, WIDTH), BF16),
            pltpu.VMEM((2, 2, WIDTH, features), BF16),
            pltpu.VMEM((2, 2, 4, 4, 32, features), F32),
            pltpu.VMEM((2, 4, 2, 2, 32, features), F32),
            pltpu.VMEM((4, 2, 2, 32, features), F32),
            pltpu.VMEM((4, 2, 2, 32, features), F32),
            dma((parts, COPIES)),
            dma((parts, COPIES)),
            dma((steps, 3)),
            dma((steps, 2, 3)),
            dma((2, 8)),
            dma((2, 8)),
            dma((2, 4)),
            dma((2, 4)),
            dma((2, 4)),
            dma((4,)),
        ],
        name="ring_sums",
        compiler_params=pltpu.CompilerParams(
            collective_id=0, has_side_effects=True, vmem_limit_bytes=62 * 2**20
        ),
    )(tokens, cotangent, w_gate, w_up, w_down)


def along_y(block, step):
    rows = lax.axis_size("row")
    return lax.ppermute(block, "row", [(r, (r + 2 * step) % rows) for r in range(rows)])


def keep_kernel(*refs):
    for src, dst in zip(refs[:3], refs[3:]):
        dst[...] = src[...]


def keep(*arrays):
    specs = [pl.BlockSpec((a.shape[0] // KEEP_PARTS, a.shape[1]), lambda i: (i, 0)) for a in arrays]
    return pl.pallas_call(
        keep_kernel,
        out_shape=tuple(jax.ShapeDtypeStruct(a.shape, a.dtype) for a in arrays),
        grid=(KEEP_PARTS,),
        in_specs=specs,
        out_specs=tuple(specs),
        name="keep",
        compiler_params=pltpu.CompilerParams(vmem_limit_bytes=62 * 2**20),
        cost_estimate=pl.CostEstimate(flops=0, transcendentals=0, bytes_accessed=sum(4 * a.size for a in arrays)),
    )(*arrays)


def shards(tokens, w_gate, w_up, w_down, cotangent):
    gate_wgrad, up_wgrad, down_wgrad, own, *sums = ring_call(tokens, w_gate, w_up, w_down, cotangent)
    came = [along_y(block, step + 1) for step, block in enumerate(sums)]
    weight_grads = keep(gate_wgrad, up_wgrad, down_wgrad)
    mixed, input_grad = (
        (own[i] + came[0][i].astype(F32) + came[1][i].astype(F32) + came[2][i].astype(F32)).astype(BF16)
        for i in range(2)
    )
    return (mixed, input_grad, *weight_grads)


def solution(mesh):
    return jax.shard_map(
        shards,
        mesh=mesh,
        in_specs=(P("row", "col"), P("col", "row"), P("col", "row"), P("row", "col"), P("row", "col")),
        out_specs=(P("row", "col"), P("row", "col"), P("col", "row"), P("col", "row"), P("row", "col")),
        check_vma=False,
    )
```

```python
import jax
import jax.numpy as jnp
from jax import lax
from jax.experimental import pallas as pl
from jax.experimental.pallas import tpu as pltpu
from jax.sharding import PartitionSpec as P

MESH = pl.DeviceIdType.MESH
BF16 = jnp.bfloat16
F32 = jnp.float32
WIDTH = 256
DEPTH = 8
EARLY = 4
AHEAD = 2
KEEP_PARTS = 2

FAR_UP, FAR_DOWN, OWN_UP, OWN_DOWN, SUM_UP, SUM_DOWN = range(6)
SECOND = 6
GIVE_UP, GIVE_DOWN, PASS_UP, PASS_DOWN = range(12, 16)
WIDE_UP, WIDE_DOWN, WIDE_PASS_UP, WIDE_PASS_DOWN = range(16, 20)
REST_UP, REST_DOWN = range(20, 22)
COPIES = 22


def dot(left, right):
    return jnp.dot(left, right, preferred_element_type=F32)


def dot_nt(left, right):
    return lax.dot_general(left, right, (((1,), (1,)), ((), ())), preferred_element_type=F32)


def dot_tn(left, right):
    return lax.dot_general(left, right, (((0,), (0,)), ((), ())), preferred_element_type=F32)


def ring_kernel(
    steps,
    tok_ref, cot_ref, wg_hbm, wu_hbm, wd_hbm,
    gg_out, ug_out, dg_out, own_out, sum1, sum2, sum3,
    wg, wu, wd, nat, perm, far, far_in, near, near_in,
    far2, far2_in, near2, near2_in, sub, all3, tok_t, grads, down_grads, acc, core_in, y_send, y_in,
    send_sem, recv_sem, w_sem, out_sem, g_send, g_recv, r_send, r_recv, y_sem, tok_sem,
):
    sum_outs = (own_out, sum1, sum2, sum3)
    row, col = lax.axis_index("row"), lax.axis_index("col")
    x, z, y, core = col // 4, col % 4, row // 2, row % 2
    width = WIDTH

    def at_x(i):
        return (row, lax.rem(i, 4) * 4 + z)

    def at_z(i):
        return (row, x * 4 + lax.rem(i, 4))

    def at_y(i):
        return (lax.rem(i, 4) * 2 + core, col)

    sibling = (row + 1 - 2 * core, col)
    rings = ((x, z, at_x, at_z), (z, x, at_z, at_x))

    own = [
        pltpu.make_async_copy(ref.at[pl.ds(32 * half, 32)], nat.at[a, y, 2 * core + half], tok_sem.at[2 * a + half])
        for a, ref in enumerate((tok_ref, cot_ref))
        for half in range(2)
    ]
    for copy in own:
        copy.start()

    barrier = pltpu.get_barrier_semaphore()
    peers = [at_x(x + 1), at_x(x + 3), at_z(z + 1), at_z(z + 3), at_y(y + 1), at_y(y + 2), at_y(y + 3), sibling]
    for peer in peers:
        pl.semaphore_signal(barrier, inc=1, device_id=peer, device_id_type=MESH)
    def fetch(k):
        cols = pl.ds(k * 2 * width, 2 * width)
        pltpu.make_async_copy(wd_hbm.at[cols, :], wd.at[k], w_sem.at[k, 2]).start()
        pltpu.make_async_copy(wg_hbm.at[:, cols], wg.at[k], w_sem.at[k, 0]).start()
        pltpu.make_async_copy(wu_hbm.at[:, cols], wu.at[k], w_sem.at[k, 1]).start()

    fetch(0)
    acc[...] = jnp.zeros_like(acc)
    pl.semaphore_wait(barrier, len(peers))

    for copy in own:
        copy.wait()

    def rows_of(a, y_at, core_at):
        return nat.at[a, y_at, pl.ds(2 * core_at, 2)]

    def y_copy(a, step, back):
        block = rows_of(a, lax.rem(y + back, 4), core)
        return pltpu.make_async_remote_copy(
            src_ref=block, dst_ref=block, send_sem=g_send.at[a, step], recv_sem=g_recv.at[a, step],
            device_id=at_y(y + step), device_id_type=MESH,
        )

    def core_copy(a, step, core_at):
        block = rows_of(a, lax.rem(y + 4 - step, 4), core_at)
        return pltpu.make_async_remote_copy(
            src_ref=block, dst_ref=block, send_sem=g_send.at[a, 4 + step], recv_sem=g_recv.at[a, 4 + step],
            device_id=sibling, device_id_type=MESH,
        )

    def gathered(a):
        for step in (0, 1, 3, 2):
            core_copy(a, step, 1 - core).wait_recv()
        for i in range(4):
            for j in range(4):
                perm[a, j, i] = nat[a, i, j]

    for a in (1, 0):
        for step in (1, 3, 2):
            y_copy(a, step, 0).start()
        core_copy(a, 0, core).start()
    for k in range(1, steps):
        fetch(k)

    def along_core(a):
        for step in (1, 3, 2):
            y_copy(a, step, 4 - step).wait_recv()
            core_copy(a, step, core).start()

    along_core(1)
    gathered(1)
    def part(h, k, a, block, first, count):
        tokens = (nat, perm)[h]
        left = tokens[1 if a == 2 else 0, block, pl.ds(first, count)].reshape(count * 32, -1)
        if a == 2:
            return dot_nt(left, wd[k, h * width : (h + 1) * width, :])
        return dot(left, (wg, wu)[a][k, :, h * width : (h + 1) * width])

    def copy_of(kind, k, h, src, dst, target):
        at = 2 * k + h
        return pltpu.make_async_remote_copy(
            src_ref=src, dst_ref=dst, send_sem=send_sem.at[at, kind], recv_sem=recv_sem.at[at, kind],
            device_id=target, device_id_type=MESH,
        )

    def copies(k, h):
        at = 2 * k + h
        p, q, at_p, at_q = rings[h]
        up, down, up2, down2 = at_p(p + 1), at_p(p + 3), at_q(q + 1), at_q(q + 3)
        q_up, q_down = lax.rem(q + 1, 4), lax.rem(q + 3, 4)
        p_up, p_down = lax.rem(p + 1, 4), lax.rem(p + 3, 4)
        table = {}

        def same(kind, src, dst, target):
            table[kind] = (src, dst, target, dst)

        for base, f, fi, n, ni, u, d in (
            (0, far, far_in, near, near_in, up, down),
            (SECOND, far2, far2_in, near2, near2_in, up2, down2),
        ):
            same(base + FAR_UP, f.at[at, 0], fi.at[at, 0], u)
            same(base + FAR_DOWN, f.at[at, 1], fi.at[at, 1], d)
            same(base + SUM_UP, n.at[at, 0, 0], ni.at[at, 0, 0], u)
            same(base + OWN_UP, n.at[at, 0, 1], ni.at[at, 0, 1], u)
            same(base + OWN_DOWN, n.at[at, 1, 0], ni.at[at, 1, 0], d)
            same(base + SUM_DOWN, n.at[at, 1, 1], ni.at[at, 1, 1], d)

        def held(kind, mine, theirs, target):
            table[kind] = (mine, mine, target, theirs)

        mine = all3.at[at, :, p, q]
        held(GIVE_UP, mine, all3.at[at, :, p, q_down], up2)
        held(GIVE_DOWN, mine, all3.at[at, :, p, q_up], down2)
        opp_q, opp_p = lax.rem(q + 2, 4), lax.rem(p + 2, 4)
        low, high = pl.ds(0, 16), pl.ds(16, 16)
        held(PASS_UP, all3.at[at, :, p, q_down, low], all3.at[at, :, p, opp_q, low], up2)
        held(PASS_DOWN, all3.at[at, :, p, q_up, high], all3.at[at, :, p, opp_q, high], down2)
        low, high = pl.ds(0, 2), pl.ds(2, 2)
        held(WIDE_UP, all3.at[at, :, p, low], all3.at[at, :, p_down, low], up)
        held(WIDE_DOWN, all3.at[at, :, p, high], all3.at[at, :, p_up, high], down)
        held(REST_UP, all3.at[at, :, p, high], all3.at[at, :, p_down, high], up)
        held(REST_DOWN, all3.at[at, :, p, low], all3.at[at, :, p_up, low], down)
        held(WIDE_PASS_UP, all3.at[at, :, p_down, low], all3.at[at, :, opp_p, low], up)
        held(WIDE_PASS_DOWN, all3.at[at, :, p_up, high], all3.at[at, :, opp_p, high], down)
        return table

    def start(k, h, *kinds, arrays=None):
        table = copies(k, h)
        for kind in kinds:
            src, dst, target, _ = table[kind]
            if arrays is not None:
                src, dst = src.at[arrays], dst.at[arrays]
            copy_of(kind, k, h, src, dst, target).start()

    def arrive(k, h, *kinds):
        table = copies(k, h)
        for kind in kinds:
            src, _, target, here = table[kind]
            copy_of(kind, k, h, here, here, target).wait_recv()

    def sent(k, h):
        for kind, (src, dst, target, _) in copies(k, h).items():
            copy_of(kind, k, h, src, dst, target).wait_send()

    def first_sums(k, h, a):
        p = rings[h][0]
        at = 2 * k + h
        whole = part(h, k, a, lax.rem(p + 2, 4), 0, 4).astype(BF16)
        far[at, 0, a] = whole[:64]
        far[at, 1, a] = whole[64:]
        near[at, 0, 1, a] = part(h, k, a, lax.rem(p + 1, 4), 2, 2).astype(BF16)
        near[at, 1, 0, a] = part(h, k, a, lax.rem(p + 3, 4), 0, 2).astype(BF16)

    firsts = (FAR_UP, FAR_DOWN, OWN_UP, OWN_DOWN)

    def hidden_grad_sums(k, send):
        cols = pl.ds(0, 2 * width)
        pltpu.make_async_copy(wd_hbm.at[cols, :], wd.at[k], w_sem.at[k, 2]).wait()
        for h in range(2):
            first_sums(k, h, 2)
            if send:
                start(k, h, *firsts, arrays=pl.ds(2, 1))

    def stage0(k):
        cols = pl.ds(0, 2 * width)

        @pl.when(k == 0)
        def _():
            for ahead in range(AHEAD):
                hidden_grad_sums(ahead, True)
                if ahead == 0:
                    along_core(0)
            gathered(0)

        @pl.when(k >= AHEAD)
        def _():
            hidden_grad_sums(k, False)

        pltpu.make_async_copy(wg_hbm.at[:, cols], wg.at[k], w_sem.at[k, 0]).wait()
        pltpu.make_async_copy(wu_hbm.at[:, cols], wu.at[k], w_sem.at[k, 1]).wait()
        for h in range(2):
            for a in range(2):
                first_sums(k, h, a)

            @pl.when(k < AHEAD)
            def _():
                start(k, h, *firsts, arrays=pl.ds(0, 2))

            @pl.when(k >= AHEAD)
            def _():
                start(k, h, *firsts)

        @pl.when(k == 3)
        def _():
            for h, tokens in enumerate((nat, perm)):
                tok_t[h] = tokens[0].reshape(tok_t.shape[1:]).T

    def stage1(k):
        for h in range(2):
            p = rings[h][0]
            at = 2 * k + h
            arrive(k, h, FAR_UP, FAR_DOWN)
            for a in range(3):
                near[at, 0, 0, a] = (
                    part(h, k, a, lax.rem(p + 1, 4), 0, 2) + far_in[at, 0, a].astype(F32)
                ).astype(BF16)
                near[at, 1, 1, a] = (
                    part(h, k, a, lax.rem(p + 3, 4), 2, 2) + far_in[at, 1, a].astype(F32)
                ).astype(BF16)
            start(k, h, SUM_UP, SUM_DOWN)

    def stage2(k):
        slot = lax.rem(k, 3)
        for h in range(2):
            p, q = rings[h][:2]
            at = 2 * k + h
            arrive(k, h, OWN_UP, OWN_DOWN, SUM_UP, SUM_DOWN)
            for a in range(3):
                for half in range(2):
                    total = (
                        part(h, k, a, p, 2 * half, 2)
                        + near_in[at, 0, half, a].astype(F32)
                        + near_in[at, 1, half, a].astype(F32)
                    )
                    sub[slot, h, a, 2 * half] = total[:32]
                    sub[slot, h, a, 2 * half + 1] = total[32:]
            for a in range(3):
                opposite = sub[slot, h, a, lax.rem(q + 2, 4)].astype(BF16)
                far2[at, 0, a] = opposite[:16]
                far2[at, 1, a] = opposite[16:]
                near2[at, 0, 1, a] = sub[slot, h, a, lax.rem(q + 1, 4), 16:, :].astype(BF16)
                near2[at, 1, 0, a] = sub[slot, h, a, lax.rem(q + 3, 4), :16, :].astype(BF16)
            start(k, h, *(SECOND + kind for kind in (FAR_UP, FAR_DOWN, OWN_UP, OWN_DOWN)))

    def stage3(k):
        slot = lax.rem(k, 3)
        for h in range(2):
            q = rings[h][1]
            at = 2 * k + h
            arrive(k, h, SECOND + FAR_UP, SECOND + FAR_DOWN)
            for a in range(3):
                near2[at, 0, 0, a] = (
                    sub[slot, h, a, lax.rem(q + 1, 4), :16, :] + far2_in[at, 0, a].astype(F32)
                ).astype(BF16)
                near2[at, 1, 1, a] = (
                    sub[slot, h, a, lax.rem(q + 3, 4), 16:, :] + far2_in[at, 1, a].astype(F32)
                ).astype(BF16)
            start(k, h, SECOND + SUM_UP, SECOND + SUM_DOWN)

    def stage4(k):
        slot = lax.rem(k, 3)
        for h in range(2):
            p, q = rings[h][:2]
            at = 2 * k + h
            arrive(k, h, *(SECOND + kind for kind in (OWN_UP, OWN_DOWN, SUM_UP, SUM_DOWN)))
            for half in range(2):
                rows = slice(16 * half, 16 * half + 16)
                gate, up, hidden_grad = (
                    sub[slot, h, a, q, rows, :]
                    + near2_in[at, 0, half, a].astype(F32)
                    + near2_in[at, 1, half, a].astype(F32)
                    for a in range(3)
                )
                sigmoid_gate = 1.0 / (1.0 + jnp.exp(-gate))
                activated = gate * sigmoid_gate
                all3[at, 0, p, q, rows, :] = (activated * up).astype(BF16)
                all3[at, 1, p, q, rows, :] = (
                    hidden_grad * up * sigmoid_gate * (1.0 + gate * (1.0 - sigmoid_gate))
                ).astype(BF16)
                all3[at, 2, p, q, rows, :] = (hidden_grad * activated).astype(BF16)
            start(k, h, GIVE_UP, GIVE_DOWN)

    def stage5(k):
        for h in range(2):
            arrive(k, h, GIVE_UP, GIVE_DOWN)
            start(k, h, PASS_UP, PASS_DOWN)

    def stage6(k):
        for h in range(2):
            arrive(k, h, PASS_UP, PASS_DOWN)
            start(k, h, WIDE_UP, WIDE_DOWN)

    def stage7(k):
        for h in range(2):
            start(k, h, REST_UP, REST_DOWN)
        for h in range(2):
            arrive(k, h, WIDE_UP, WIDE_DOWN)
            start(k, h, WIDE_PASS_UP, WIDE_PASS_DOWN)

    def grad_copies(k):
        slot = lax.rem(k, 2)
        copies_out = []
        for h in range(2):
            span = pl.ds(pl.multiple_of((2 * k + h) * width, width), width)
            for a, (out, src) in enumerate(
                ((gg_out.at[:, span], grads.at[slot, h, 0]), (ug_out.at[:, span], grads.at[slot, h, 1]),
                 (dg_out.at[span, :], down_grads.at[slot, h]))
            ):
                copies_out.append(pltpu.make_async_copy(src, out, out_sem.at[k, h, a]))
        return copies_out

    def stage9(k):
        slot = lax.rem(k, 2)

        @pl.when(k >= 2)
        def _():
            for copy in grad_copies(k - 2):
                copy.wait()

        for h in range(2):
            at = 2 * k + h
            sent(k, h)
            for a in range(2):
                grads[slot, h, a] = dot(tok_t[h], all3[at, 1 + a].reshape(512, width)).astype(BF16)
            cot_all = (nat, perm)[h][1].reshape(512, -1)
            down_grads[slot, h] = dot_tn(all3[at, 0].reshape(512, width), cot_all).astype(BF16)
        for copy in grad_copies(k):
            copy.start()

    def stage8(k):
        late = (k >= EARLY).astype(jnp.int32)
        for last in range(2):
            for h in range(2):
                at = 2 * k + h
                hidden_rows = slice(h * width, (h + 1) * width)
                for ahead in (2,) if last else (0, 1, 3):
                    if ahead == 1:
                        arrive(k, h, REST_UP, REST_DOWN)
                    if ahead == 2:
                        arrive(k, h, WIDE_PASS_UP, WIDE_PASS_DOWN)
                    b = lax.rem(rings[h][0] + ahead, 4)
                    hidden, gate_grad, up_grad = (all3[at, a, b].reshape(128, width) for a in range(3))
                    mixed = dot(hidden, wd[k, hidden_rows, :])
                    into = dot_nt(gate_grad, wg[k, :, hidden_rows]) + dot_nt(up_grad, wu[k, :, hidden_rows])
                    for j in range(4):
                        rows = slice(32 * j, 32 * j + 32)
                        i, jj = (b, j) if h == 0 else (j, b)
                        acc[late, 0, i, jj] += mixed[rows]
                        acc[late, 1, i, jj] += into[rows]

    order = (2, 1, 3, 0)

    def core_sum(late, step):
        block = acc.at[late, :, lax.rem(y + step, 4), pl.ds(2 * (1 - core), 2)]
        return pltpu.make_async_remote_copy(
            src_ref=block, dst_ref=core_in.at[late, step], send_sem=r_send.at[late, step],
            recv_sem=r_recv.at[late, step], device_id=sibling, device_id_type=MESH,
        )

    def chip_sum(late, step):
        core_sum(late, step).wait_recv()
        return acc[late, :, lax.rem(y + step, 4), pl.ds(2 * core, 2)] + core_in[late, step]

    def y_sum(step):
        return pltpu.make_async_remote_copy(
            src_ref=y_send.at[step], dst_ref=y_in.at[step], send_sem=y_sem.at[0, step], recv_sem=y_sem.at[1, step],
            device_id=at_y(y + step), device_id_type=MESH,
        )

    stages = (stage0, stage1, stage2, stage3, stage4, stage5, stage6, stage7, stage8)

    def turn(i, carry):
        for late, stage in enumerate(stages):
            @pl.when((i >= late) & (i < steps + late))
            def _():
                stage(i - late)

        @pl.when(i == EARLY + DEPTH - 1)
        def _():
            for step in order:
                core_sum(0, step).start()

        @pl.when(i == steps + DEPTH - 1)
        def _():
            for step in order:
                core_sum(1, step).start()

        @pl.when(i >= DEPTH)
        def _():
            stage9(i - DEPTH)

        @pl.when(i == EARLY + DEPTH - 1)
        def _():
            for step in order:
                y_send[step] = chip_sum(0, step)
                if step:
                    y_sum(step).start()
        return carry

    lax.fori_loop(0, steps + DEPTH, turn, 0)

    for step in order[:3]:
        total = chip_sum(1, step)
        for j in range(2):
            sum_outs[step][:, 32 * j : 32 * j + 32, :] = total[:, j].astype(BF16)
    total = chip_sum(1, 0) + y_send[0]
    for step in (1, 3, 2):
        y_sum(step).wait_recv()
        total += y_in[step]
    for j in range(2):
        own_out[:, 32 * j : 32 * j + 32, :] = total[:, j]
    for step in order:
        for late in range(2):
            core_sum(late, step).wait_send()
        if step:
            y_sum(step).wait_send()
    for a in range(2):
        for step in (1, 2, 3):
            y_copy(a, step, 0).wait_send()
        for step in range(4):
            core_copy(a, step, core).wait_send()

    for k in (steps - 2, steps - 1):
        for copy in grad_copies(k):
            copy.wait()


def ring_call(tokens, w_gate, w_up, w_down, cotangent):
    features, hidden = w_gate.shape
    steps = hidden // (2 * WIDTH)
    parts = 2 * steps
    any_space = pl.BlockSpec(memory_space=pl.ANY)
    vmem = pl.BlockSpec(memory_space=pltpu.VMEM)

    def kernel(*refs):
        ring_kernel(steps, *refs)

    wide = jax.ShapeDtypeStruct((features, hidden), BF16)
    tall = jax.ShapeDtypeStruct((hidden, features), BF16)
    dma = pltpu.SemaphoreType.DMA
    return pl.pallas_call(
        kernel,
        out_shape=(wide, wide, tall) + (jax.ShapeDtypeStruct((2, 64, features), F32),)
        + (jax.ShapeDtypeStruct((2, 64, features), BF16),) * 3,
        in_specs=[any_space] * 5,
        out_specs=(any_space,) * 3 + (vmem,) * 4,
        scratch_shapes=[
            pltpu.VMEM((steps, features, 2 * WIDTH), BF16),
            pltpu.VMEM((steps, features, 2 * WIDTH), BF16),
            pltpu.VMEM((steps, 2 * WIDTH, features), BF16),
            pltpu.VMEM((2, 4, 4, 32, features), BF16),
            pltpu.VMEM((2, 4, 4, 32, features), BF16),
            pltpu.VMEM((parts, 2, 3, 64, WIDTH), BF16),
            pltpu.VMEM((parts, 2, 3, 64, WIDTH), BF16),
            pltpu.VMEM((parts, 2, 2, 3, 64, WIDTH), BF16),
            pltpu.VMEM((parts, 2, 2, 3, 64, WIDTH), BF16),
            pltpu.VMEM((parts, 2, 3, 16, WIDTH), BF16),
            pltpu.VMEM((parts, 2, 3, 16, WIDTH), BF16),
            pltpu.VMEM((parts, 2, 2, 3, 16, WIDTH), BF16),
            pltpu.VMEM((parts, 2, 2, 3, 16, WIDTH), BF16),
            pltpu.VMEM((3, 2, 3, 4, 32, WIDTH), F32),
            pltpu.VMEM((parts, 3, 4, 4, 32, WIDTH), BF16),
            pltpu.VMEM((2, features, 512), BF16),
            pltpu.VMEM((2, 2, 2, features, WIDTH), BF16),
            pltpu.VMEM((2, 2, WIDTH, features), BF16),
            pltpu.VMEM((2, 2, 4, 4, 32, features), F32),
            pltpu.VMEM((2, 4, 2, 2, 32, features), F32),
            pltpu.VMEM((4, 2, 2, 32, features), F32),
            pltpu.VMEM((4, 2, 2, 32, features), F32),
            dma((parts, COPIES)),
            dma((parts, COPIES)),
            dma((steps, 3)),
            dma((steps, 2, 3)),
            dma((2, 8)),
            dma((2, 8)),
            dma((2, 4)),
            dma((2, 4)),
            dma((2, 4)),
            dma((4,)),
        ],
        name="ring_sums",
        compiler_params=pltpu.CompilerParams(
            collective_id=0, has_side_effects=True, vmem_limit_bytes=62 * 2**20
        ),
    )(tokens, cotangent, w_gate, w_up, w_down)


def along_y(block, step):
    rows = lax.axis_size("row")
    return lax.ppermute(block, "row", [(r, (r + 2 * step) % rows) for r in range(rows)])


def keep_kernel(*refs):
    for src, dst in zip(refs[:3], refs[3:]):
        dst[...] = src[...]


def keep(*arrays):
    specs = [pl.BlockSpec((a.shape[0] // KEEP_PARTS, a.shape[1]), lambda i: (i, 0)) for a in arrays]
    return pl.pallas_call(
        keep_kernel,
        out_shape=tuple(jax.ShapeDtypeStruct(a.shape, a.dtype) for a in arrays),
        grid=(KEEP_PARTS,),
        in_specs=specs,
        out_specs=tuple(specs),
        name="keep",
        compiler_params=pltpu.CompilerParams(vmem_limit_bytes=62 * 2**20),
        cost_estimate=pl.CostEstimate(flops=0, transcendentals=0, bytes_accessed=sum(4 * a.size for a in arrays)),
    )(*arrays)


def shards(tokens, w_gate, w_up, w_down, cotangent):
    gate_wgrad, up_wgrad, down_wgrad, own, *sums = ring_call(tokens, w_gate, w_up, w_down, cotangent)
    came = [along_y(block, step + 1) for step, block in enumerate(sums)]
    weight_grads = keep(gate_wgrad, up_wgrad, down_wgrad)
    mixed, input_grad = (
        (own[i] + came[0][i].astype(F32) + came[1][i].astype(F32) + came[2][i].astype(F32)).astype(BF16)
        for i in range(2)
    )
    return (mixed, input_grad, *weight_grads)


def solution(mesh):
    return jax.shard_map(
        shards,
        mesh=mesh,
        in_specs=(P("row", "col"), P("col", "row"), P("col", "row"), P("row", "col"), P("row", "col")),
        out_specs=(P("row", "col"), P("row", "col"), P("col", "row"), P("col", "row"), P("row", "col")),
        check_vma=False,
    )
```
